32 devices in a mesh: groups: 2 (over y), seq: 8 (over z, x), heads: 2 (over core).
Axes of the slice: x: 2, y: 2, z: 4, core: 2. Of those that a mesh axis runs over, the one named last changes fastest.
Arguments:
- queries: bfloat16 [4096, 2048], P(('groups', 'seq'), 'heads'), parts along dimension 0, may hold values from -180 to 180
- key_rows: bfloat16 [4096, 2048], P(('groups', 'seq'), 'heads'), parts along dimension 0, may hold values from -6 to 6
- value_rows: bfloat16 [4096, 2048], P(('groups', 'seq'), 'heads'), parts along dimension 0, may hold values from -19 to 19
- query_basis: bfloat16 [4096, 256], P(('groups', 'seq'), 'heads'), parts along dimension 0, may hold values from -6 to 6
- key_basis: bfloat16 [4096, 256], P(('groups', 'seq'), 'heads'), parts along dimension 0, may hold values from -6 to 6
- linear_gain: float32 [2048], P('heads'), may hold values from 0.25 to 1.75
Outputs:
- layer_output: bfloat16 [4096, 2048], P(('groups', 'seq'), 'heads'), parts along dimension 0
The draws below stay inside these ranges and needn't reach their ends.
There are 2 independent parts, one for each index of `groups`. The reference program is written for one: setup_inputs(seed, part) draws one part's arguments, and reference() takes and returns one part's arrays. A program takes and returns all parts, laid end to end along the dimension named above; an argument that names none is the same for every part. Nothing has to cross between parts.
All inputs are finite; a program needn't handle non-finite values.
Results may differ from the reference program's by a relative error of at most 0.0075.
Values may be sent and summed in bfloat16 or wider, within the bound.
A program may use at most 320 MiB of HBM per device.

```python
import math
import jax
import jax.numpy as jnp
from jax import lax

DH = 128
HEADS = 16
FD = 16
WINDOW = 256
TOK_DEV = 256
FEAT = 273
TOKENS = 2048


def paired_rows(key):
    base = jax.random.fold_in(key, 11)
    query_key, row_key = jax.random.split(base, 2)
    shape = (TOKENS, HEADS * DH)
    key_vals = jnp.clip(jax.random.normal(row_key, shape, jnp.float32), -6.0, 6.0)
    query_vals = jnp.clip(jax.random.normal(query_key, shape, jnp.float32) * 1.5, -9.0, 9.0)
    return (query_vals, key_vals)


def draw_queries(key, part):
    return paired_rows(key)[0].astype(jnp.bfloat16)


def draw_key_rows(key, part):
    return paired_rows(key)[1].astype(jnp.bfloat16)


def draw_value_rows(key, part):
    base = jax.random.fold_in(key, 23)
    noise_key, scale_key = jax.random.split(base, 2)
    shape = (TOKENS, HEADS * DH)
    column_scale = jnp.exp(jax.random.uniform(scale_key, (HEADS * DH,), jnp.float32, math.log(0.3), math.log(3.0)))
    noise = jnp.clip(jax.random.normal(noise_key, shape, jnp.float32), -6.0, 6.0)
    values_out = noise
    return (values_out * column_scale[None, :]).astype(jnp.bfloat16)


def level_of(key, dims, cuts, smallest, high):
    factor_of = 1.0
    for axis_at, shards_of in cuts:
        steps = jax.random.uniform(jax.random.fold_in(jax.random.fold_in(key, 6), axis_at), (shards_of,), jnp.float32, smallest / len(cuts), high / len(cuts))
        factor_of = factor_of * jnp.repeat(jnp.exp(steps), dims[axis_at] // shards_of).reshape((-1,) + (1,) * (len(dims) - 1 - axis_at))
    return factor_of


def normal_values(own_key, extent, width, bound, cuts=(), kind=jnp.bfloat16):
    values = jax.random.normal(own_key, extent, jnp.float32) * width
    if len(cuts) > 0:
        values = level_of(own_key, extent, cuts, -0.22, 0.18) * values
    return jnp.clip(values, min=-bound, max=bound).astype(kind)


def setup_inputs(seed: int = 0, part: int = 0) -> dict:
    keys = jax.random.split(jax.random.key(seed), 7)
    part_keys = jax.random.split(jax.random.fold_in(keys[6], part), 7)
    queries = draw_queries(jax.random.fold_in(jax.random.fold_in(keys[6], part), 71), part)
    key_rows = draw_key_rows(jax.random.fold_in(jax.random.fold_in(keys[6], part), 71), part)
    value_rows = draw_value_rows(jax.random.fold_in(jax.random.fold_in(keys[6], part), 71), part)
    query_basis = normal_values(part_keys[3], (TOKENS, HEADS * FD), 1.0, 6.0, ((0, 8), (1, 2)))
    key_basis = normal_values(part_keys[4], (TOKENS, HEADS * FD), 1.0, 6.0, ((0, 8), (1, 2)))
    linear_gain = jnp.clip(1.0 + 0.15 * jax.random.normal(keys[5], (HEADS * DH,), jnp.float32), 0.25, 1.75)
    return dict(queries=queries, key_rows=key_rows, value_rows=value_rows, query_basis=query_basis, key_basis=key_basis, linear_gain=linear_gain)


def feature_map(basis):
    count = basis.shape[0]
    scaled = basis.astype(jnp.float32).reshape(count, HEADS, FD).transpose(1, 2, 0) * FD ** (-0.25)
    second = (scaled[:, :, None, :] * scaled[:, None, :, :]).reshape(HEADS, FD * FD, count) / math.sqrt(2.0)
    ones_row = jnp.ones((HEADS, 1, count), jnp.float32)
    joined = jnp.concatenate([ones_row, scaled, second], axis=1)
    return lax.optimization_barrier(joined.astype(jnp.bfloat16)).astype(jnp.float32)

def reference(queries, key_rows, value_rows, query_basis, key_basis, linear_gain):
    blocks = TOKENS // TOK_DEV
    query_blocks = query_basis.reshape(blocks, TOK_DEV, HEADS * FD)
    key_blocks = key_basis.reshape(blocks, TOK_DEV, HEADS * FD)
    value_blocks = value_rows.reshape(blocks, TOK_DEV, HEADS * DH)
    causal = jnp.arange(TOK_DEV)[:, None] >= jnp.arange(TOK_DEV)[None, :]

    def linear_step(carry_state, segment):
        query_part, key_part, value_part = segment
        query_feats = feature_map(query_part)
        key_feats = feature_map(key_part)
        value_heads = value_part.astype(jnp.float32).reshape(TOK_DEV, HEADS, DH)
        prior = lax.optimization_barrier(carry_state.astype(jnp.bfloat16)).astype(jnp.float32)
        cross = jnp.einsum('hft,hfd->htd', query_feats, prior)
        query_heads = query_part.astype(jnp.float32).reshape(TOK_DEV, HEADS, FD)
        key_heads = key_part.astype(jnp.float32).reshape(TOK_DEV, HEADS, FD)
        affinity = jnp.einsum('thf,shf->hts', query_heads, key_heads) / math.sqrt(FD)
        kernel = jnp.where(causal, 1.0 + affinity + affinity * affinity / 2.0, 0.0)
        kernel = lax.optimization_barrier(kernel.astype(jnp.bfloat16)).astype(jnp.float32)
        local_part = jnp.einsum('hts,shd->htd', kernel, value_heads)
        new_state = carry_state + jnp.einsum('hft,thd->hfd', key_feats, value_heads)
        return (new_state, cross + local_part)
    start_state = jnp.zeros((HEADS, FEAT, DH), jnp.float32)
    final_state, raws = lax.scan(linear_step, start_state, (query_blocks, key_blocks, value_blocks))
    linear_raw = raws.transpose(0, 2, 1, 3).reshape(TOKENS, HEADS, DH)
    scale_inv = lax.rsqrt(lax.optimization_barrier(jnp.mean(linear_raw * linear_raw, axis=-1, keepdims=True)) + 1e-05)
    linear_out = linear_raw * scale_inv * linear_gain.reshape(HEADS, DH)[None, :, :]
    padded_keys = jnp.concatenate([jnp.zeros((WINDOW, HEADS * DH), jnp.bfloat16), key_rows], axis=0)
    padded_values = jnp.concatenate([jnp.zeros((WINDOW, HEADS * DH), jnp.bfloat16), value_rows], axis=0)
    query_pos = jnp.arange(WINDOW, dtype=jnp.int32)[:, None]
    key_pos = jnp.arange(2 * WINDOW, dtype=jnp.int32)[None, :]
    inside = (key_pos >= query_pos) & (key_pos <= query_pos + WINDOW)

    def window_block(block_index):
        begin = (block_index * WINDOW).astype(jnp.int32)
        query_tile = lax.dynamic_slice_in_dim(queries, begin, WINDOW, 0).astype(jnp.float32).reshape(WINDOW, HEADS, DH)
        key_tile = lax.dynamic_slice_in_dim(padded_keys, begin, 2 * WINDOW, 0).astype(jnp.float32).reshape(2 * WINDOW, HEADS, DH)
        value_tile = lax.dynamic_slice_in_dim(padded_values, begin, 2 * WINDOW, 0).astype(jnp.float32).reshape(2 * WINDOW, HEADS, DH)
        scores = jnp.einsum('thd,shd->hts', query_tile, key_tile) / math.sqrt(DH)
        allowed = inside & (begin - WINDOW + key_pos >= 0)
        scores = jnp.where(allowed[None, :, :], scores, -1e+30)
        row_top = lax.optimization_barrier(jnp.max(scores, axis=-1, keepdims=True))
        expo = jnp.exp(scores - row_top)
        row_total = lax.optimization_barrier(jnp.sum(expo, axis=-1, keepdims=True))
        weights = lax.optimization_barrier(expo.astype(jnp.bfloat16)).astype(jnp.float32)
        return jnp.einsum('hts,shd->htd', weights, value_tile) / row_total
    tiles = lax.map(window_block, jnp.arange(TOKENS // WINDOW, dtype=jnp.int32))
    window_out = tiles.transpose(0, 2, 1, 3).reshape(TOKENS, HEADS, DH)
    return (window_out + linear_out).reshape(TOKENS, HEADS * DH).astype(jnp.bfloat16)
```

```python
import functools
import math

import jax
import jax.numpy as jnp
from jax import lax
from jax.experimental import pallas as pl
from jax.experimental.pallas import tpu as pltpu
from jax.sharding import PartitionSpec as P

DH = 128
FD = 16
ROWS = 160
ONE = 136
LIN = 144
NEG = -1e30
F32 = jnp.float32
BF16 = jnp.bfloat16


def dot_nn(a, b):
    return lax.dot_general(a, b, (((1,), (0,)), ((), ())), preferred_element_type=F32)


def dot_nt(a, b):
    return lax.dot_general(a, b, (((1,), (1,)), ((), ())), preferred_element_type=F32)


def pair_places(c):
    i = c % FD
    j = (i + c // FD) % FD
    return i, j


def entry_scale(c, doubled):
    pair = 0.25 / math.sqrt(2.0)
    off = 2.0 * pair if doubled else pair
    scale = jnp.where(c < FD, pair, off)
    scale = jnp.where(c >= ONE, 0.0, scale)
    scale = jnp.where(c == ONE, 1.0, scale)
    return jnp.where(c >= LIN, 0.5, scale).astype(F32)


def kernel(n, heads, q_ref, k_ref, v_ref, qb_ref, kb_ref, gain_ref, out_ref,
           khalo, vhalo, prior, onward, state, qfeat, top, total, owin, lin,
           ksend, vsend, psend, krecv, vrecv, precv):
    me = lax.axis_index("seq")
    tokens = q_ref.shape[0]
    has_next = me < n - 1
    has_prev = me > 0
    nxt = {"seq": jnp.minimum(me + 1, n - 1)}
    prv = {"seq": jnp.maximum(me - 1, 0)}

    barrier = pltpu.get_barrier_semaphore()

    @pl.when(has_prev)
    def _():
        pl.semaphore_signal(barrier, inc=1, device_id=prv, device_id_type=pl.DeviceIdType.MESH)

    @pl.when(me == 0)
    def _():
        khalo[...] = jnp.zeros_like(khalo)
        vhalo[...] = jnp.zeros_like(vhalo)
        prior[...] = jnp.zeros_like(prior)

    @pl.when(has_next)
    def _():
        pl.semaphore_wait(barrier, 1)

    def cols(h):
        return pl.ds(pl.multiple_of(h * DH, DH), DH)

    def kcopy(h):
        return pltpu.make_async_remote_copy(
            src_ref=k_ref.at[:, cols(h)], dst_ref=khalo.at[h], send_sem=ksend.at[h],
            recv_sem=krecv.at[h], device_id=nxt, device_id_type=pl.DeviceIdType.MESH)

    def vcopy(h):
        return pltpu.make_async_remote_copy(
            src_ref=v_ref.at[:, cols(h)], dst_ref=vhalo.at[h], send_sem=vsend.at[h],
            recv_sem=vrecv.at[h], device_id=nxt, device_id_type=pl.DeviceIdType.MESH)

    def pcopy(h):
        return pltpu.make_async_remote_copy(
            src_ref=onward.at[h], dst_ref=prior.at[h], send_sem=psend.at[h],
            recv_sem=precv.at[h], device_id=nxt, device_id_type=pl.DeviceIdType.MESH)

    def each_head(body):
        def step(h, carry):
            body(h)
            return carry
        lax.fori_loop(0, heads, step, 0)

    crow = lax.broadcasted_iota(jnp.int32, (ROWS, heads * FD), 0)
    lane = lax.broadcasted_iota(jnp.int32, (ROWS, heads * FD), 1)
    i, j = pair_places(crow)
    first = jnp.where(crow == ONE, -1, lane - i)
    second = jnp.where(crow >= ONE, -1, lane - j)
    ccol = lax.broadcasted_iota(jnp.int32, (ROWS, 1), 0)
    kscale = entry_scale(ccol, False)
    kone_a = jnp.where(ccol == ONE, 1.0, 0.0).astype(F32)
    kone_b = jnp.where(ccol >= ONE, 1.0, 0.0).astype(F32)

    def own_state(h):
        pick_a = jnp.where(first == h * FD, 1.0, 0.0).astype(BF16)
        pick_b = jnp.where(second == h * FD, 1.0, 0.0).astype(BF16)
        a = dot_nt(pick_a, kb_ref[...]) + kone_a
        b = dot_nt(pick_b, kb_ref[...]) + kone_b
        feats = (a * b * kscale).astype(BF16)
        got = dot_nn(feats, v_ref[:, cols(h)])
        state[h] = got

        @pl.when(me == 0)
        def _():
            onward[h] = got.astype(onward.dtype)
            pcopy(h).start()

    each_head(own_state)

    @pl.when(has_next)
    def _():
        def send(h):
            kcopy(h).start()
            vcopy(h).start()
        each_head(send)

    def chain(h):
        pcopy(h).wait_recv()

        @pl.when(has_next)
        def _():
            onward[h] = (prior[h].astype(F32) + state[h]).astype(onward.dtype)
            pcopy(h).start()

    early = n // 2 - 1

    @pl.when(has_prev & (me <= early))
    def _():
        each_head(chain)

    row = lax.broadcasted_iota(jnp.int32, (tokens, tokens), 0)
    col = lax.broadcasted_iota(jnp.int32, (tokens, tokens), 1)
    qrow = lax.broadcasted_iota(jnp.int32, (heads * FD, ROWS), 1)
    qlane = lax.broadcasted_iota(jnp.int32, (heads * FD, ROWS), 0)
    qi, qj = pair_places(qrow)
    qfirst = jnp.where(qrow == ONE, -1, qlane - qi)
    qsecond = jnp.where(qrow >= ONE, -1, qlane - qj)
    clane = lax.broadcasted_iota(jnp.int32, (1, ROWS), 1)
    qscale = entry_scale(clane, True)
    qone_a = jnp.where(clane == ONE, 1.0, 0.0).astype(F32)
    qone_b = jnp.where(clane >= ONE, 1.0, 0.0).astype(F32)
    blane = lax.broadcasted_iota(jnp.int32, (1, heads * FD), 1) // FD
    root = 1.0 / math.sqrt(DH)

    def local(h):
        v = v_ref[:, cols(h)]
        scores = dot_nt(q_ref[:, cols(h)], k_ref[:, cols(h)]) * root
        scores = jnp.where(col <= row, scores, NEG)
        peak = jnp.max(scores, axis=-1, keepdims=True)
        expo = jnp.exp(scores - peak)
        top[h] = peak
        total[h] = jnp.sum(expo, axis=-1, keepdims=True)
        owin[h] = dot_nn(expo.astype(BF16), v)
        qb = qb_ref[...]
        mine = jnp.where(blane == h, 1.0, 0.0).astype(BF16)
        w = dot_nt(qb * mine, kb_ref[...]) * (1.0 / math.sqrt(FD))
        kern = jnp.where(col <= row, 1.0 + w + w * w * 0.5, 0.0).astype(BF16)
        lin[h] = dot_nn(kern, v)
        pick_a = jnp.where(qfirst == h * FD, 1.0, 0.0).astype(BF16)
        pick_b = jnp.where(qsecond == h * FD, 1.0, 0.0).astype(BF16)
        a = dot_nn(qb, pick_a) + qone_a
        b = dot_nn(qb, pick_b) + qone_b
        qfeat[h] = (a * b * qscale).astype(BF16)

    each_head(local)

    @pl.when(me > early)
    def _():
        each_head(chain)

    reach = jnp.where(has_prev, 0, tokens)

    def finish(h):
        @pl.when(has_prev)
        def _():
            kcopy(h).wait_recv()
            vcopy(h).wait_recv()

        scores = dot_nt(q_ref[:, cols(h)], khalo[h]) * root
        scores = jnp.where(col >= row + reach, scores, NEG)
        before = top[h]
        peak = jnp.maximum(before, jnp.max(scores, axis=-1, keepdims=True))
        expo = jnp.exp(scores - peak)
        shrink = jnp.exp(before - peak)
        full = total[h] * shrink + jnp.sum(expo, axis=-1, keepdims=True)
        window = (owin[h] * shrink + dot_nn(expo.astype(BF16), vhalo[h])) / full
        raw = lin[h] + dot_nn(qfeat[h], prior[h].astype(BF16))
        inv = lax.rsqrt(jnp.mean(raw * raw, axis=-1, keepdims=True) + 1e-05)
        out_ref[:, cols(h)] = (window + raw * inv * gain_ref[:, cols(h)]).astype(BF16)

    each_head(finish)

    @pl.when(has_next)
    def _():
        def sent(h):
            kcopy(h).wait_send()
            vcopy(h).wait_send()
            pcopy(h).wait_send()
        each_head(sent)


def solution(mesh):
    n = mesh.shape["seq"]
    carried = BF16 if n <= 16 else F32

    def on_device(queries, key_rows, value_rows, query_basis, key_basis, linear_gain):
        tokens, width = queries.shape
        heads = width // DH
        vmem = pl.BlockSpec(memory_space=pltpu.VMEM)
        dma = pltpu.SemaphoreType.DMA((heads,))
        flops = 2 * tokens * heads * DH * (4 * tokens + tokens + 2 * ROWS + 4 * ROWS)
        return pl.pallas_call(
            functools.partial(kernel, n, heads),
            out_shape=jax.ShapeDtypeStruct((tokens, width), BF16),
            in_specs=[vmem] * 6,
            out_specs=vmem,
            scratch_shapes=[
                pltpu.VMEM((heads, tokens, DH), BF16),
                pltpu.VMEM((heads, tokens, DH), BF16),
                pltpu.VMEM((heads, ROWS, DH), carried),
                pltpu.VMEM((heads, ROWS, DH), carried),
                pltpu.VMEM((heads, ROWS, DH), F32),
                pltpu.VMEM((heads, tokens, ROWS), BF16),
                pltpu.VMEM((heads, tokens, 1), F32),
                pltpu.VMEM((heads, tokens, 1), F32),
                pltpu.VMEM((heads, tokens, DH), F32),
                pltpu.VMEM((heads, tokens, DH), F32),
                dma, dma, dma, dma, dma, dma,
            ],
            compiler_params=pltpu.CompilerParams(
                collective_id=0, has_side_effects=True, vmem_limit_bytes=40 * 2**20),
            cost_estimate=pl.CostEstimate(
                flops=flops, bytes_accessed=8 * tokens * width, transcendentals=2 * tokens * tokens * heads),
        )(queries, key_rows, value_rows, query_basis, key_basis, linear_gain.reshape(1, width))

    rows = P(("groups", "seq"), "heads")
    return jax.shard_map(
        on_device,
        mesh=mesh,
        in_specs=(rows, rows, rows, rows, rows, P("heads")),
        out_specs=rows,
        check_vma=False,
    )
```

```python
import functools
import math

import jax
import jax.numpy as jnp
from jax import lax
from jax.experimental import pallas as pl
from jax.experimental.pallas import tpu as pltpu
from jax.sharding import PartitionSpec as P

DH = 128
FD = 16
ROWS = 160
ONE = 136
LIN = 144
NEG = -1e30
F32 = jnp.float32
BF16 = jnp.bfloat16


def dot_nn(a, b):
    return lax.dot_general(a, b, (((1,), (0,)), ((), ())), preferred_element_type=F32)


def dot_nt(a, b):
    return lax.dot_general(a, b, (((1,), (1,)), ((), ())), preferred_element_type=F32)


def pair_places(c):
    i = c % FD
    j = (i + c // FD) % FD
    return i, j


def entry_scale(c, doubled):
    pair = 0.25 / math.sqrt(2.0)
    off = 2.0 * pair if doubled else pair
    scale = jnp.where(c < FD, pair, off)
    scale = jnp.where(c >= ONE, 0.0, scale)
    scale = jnp.where(c == ONE, 1.0, scale)
    return jnp.where(c >= LIN, 0.5, scale).astype(F32)


def kernel(n, heads, q_hbm, k_hbm, v_hbm, qb_hbm, kb_hbm, gain_hbm, out_ref,
           q_ref, k_ref, v_ref, qb_ref, kb_ref, gain_ref, loads, khalo, vhalo, prior, onward, state, qfeat, top, total, owin, lin,
           ksend, vsend, psend, krecv, vrecv, precv):
    me = lax.axis_index("seq")
    tokens = q_ref.shape[0]
    has_next = me < n - 1
    has_prev = me > 0
    nxt = {"seq": jnp.minimum(me + 1, n - 1)}
    prv = {"seq": jnp.maximum(me - 1, 0)}

    pairs = ((kb_hbm, kb_ref), (v_hbm, v_ref), (k_hbm, k_ref), (qb_hbm, qb_ref), (q_hbm, q_ref),
             (gain_hbm, gain_ref))
    fetches = [pltpu.make_async_copy(a, b, loads.at[at]) for at, (a, b) in enumerate(pairs)]
    barrier = pltpu.get_barrier_semaphore()

    @pl.when(has_prev)
    def _():
        pl.semaphore_signal(barrier, inc=1, device_id=prv, device_id_type=pl.DeviceIdType.MESH)

    for fetch in fetches:
        fetch.start()

    @pl.when(me == 0)
    def _():
        khalo[...] = jnp.zeros_like(khalo)
        vhalo[...] = jnp.zeros_like(vhalo)
        prior[...] = jnp.zeros_like(prior)

    @pl.when(has_next)
    def _():
        pl.semaphore_wait(barrier, 1)

    def cols(h):
        return pl.ds(h * DH, DH)

    def kcopy(h):
        return pltpu.make_async_remote_copy(
            src_ref=k_hbm.at[:, cols(h)], dst_ref=khalo.at[h], send_sem=ksend.at[h],
            recv_sem=krecv.at[h], device_id=nxt, device_id_type=pl.DeviceIdType.MESH)

    def vcopy(h):
        return pltpu.make_async_remote_copy(
            src_ref=v_hbm.at[:, cols(h)], dst_ref=vhalo.at[h], send_sem=vsend.at[h],
            recv_sem=vrecv.at[h], device_id=nxt, device_id_type=pl.DeviceIdType.MESH)

    def pcopy(h):
        return pltpu.make_async_remote_copy(
            src_ref=onward.at[h], dst_ref=prior.at[h], send_sem=psend.at[h],
            recv_sem=precv.at[h], device_id=nxt, device_id_type=pl.DeviceIdType.MESH)

    def each_head(body):
        for h in range(heads):
            body(h)

    crow = lax.broadcasted_iota(jnp.int32, (ROWS, heads * FD), 0)
    lane = lax.broadcasted_iota(jnp.int32, (ROWS, heads * FD), 1)
    i, j = pair_places(crow)
    first = jnp.where(crow == ONE, -1, lane - i)
    second = jnp.where(crow >= ONE, -1, lane - j)
    ccol = lax.broadcasted_iota(jnp.int32, (ROWS, 1), 0)
    kscale = entry_scale(ccol, False)
    kone_a = jnp.where(ccol == ONE, 1.0, 0.0).astype(F32)
    kone_b = jnp.where(ccol >= ONE, 1.0, 0.0).astype(F32)

    def own_state(h):
        pick_a = jnp.where(first == h * FD, 1.0, 0.0).astype(BF16)
        pick_b = jnp.where(second == h * FD, 1.0, 0.0).astype(BF16)
        a = dot_nt(pick_a, kb_ref[...]) + kone_a
        b = dot_nt(pick_b, kb_ref[...]) + kone_b
        feats = (a * b * kscale).astype(BF16)
        state[h] = dot_nn(feats, v_ref[:, cols(h)])

    fetches[0].wait()
    fetches[1].wait()
    each_head(own_state)

    @pl.when(me == 0)
    def _():
        def send(h):
            onward[h] = state[h].astype(onward.dtype)
            pcopy(h).start()
        each_head(send)

    @pl.when(has_next)
    def _():
        def send(h):
            kcopy(h).start()
            vcopy(h).start()
        each_head(send)

    def chain(h):
        pcopy(h).wait_recv()

        @pl.when(has_next)
        def _():
            onward[h] = (prior[h].astype(F32) + state[h]).astype(onward.dtype)
            pcopy(h).start()

    early = n // 2 - 1

    @pl.when(has_prev & (me <= early))
    def _():
        each_head(chain)

    row = lax.broadcasted_iota(jnp.int32, (tokens, tokens), 0)
    col = lax.broadcasted_iota(jnp.int32, (tokens, tokens), 1)
    qrow = lax.broadcasted_iota(jnp.int32, (heads * FD, ROWS), 1)
    qlane = lax.broadcasted_iota(jnp.int32, (heads * FD, ROWS), 0)
    qi, qj = pair_places(qrow)
    qfirst = jnp.where(qrow == ONE, -1, qlane - qi)
    qsecond = jnp.where(qrow >= ONE, -1, qlane - qj)
    clane = lax.broadcasted_iota(jnp.int32, (1, ROWS), 1)
    qscale = entry_scale(clane, True)
    qone_a = jnp.where(clane == ONE, 1.0, 0.0).astype(F32)
    qone_b = jnp.where(clane >= ONE, 1.0, 0.0).astype(F32)
    blane = lax.broadcasted_iota(jnp.int32, (1, heads * FD), 1) // FD
    root = 1.0 / math.sqrt(DH)

    def local(h):
        v = v_ref[:, cols(h)]
        scores = dot_nt(q_ref[:, cols(h)], k_ref[:, cols(h)]) * root
        scores = jnp.where(col <= row, scores, NEG)
        peak = jnp.max(scores, axis=-1, keepdims=True)
        expo = jnp.exp(scores - peak)
        top[h] = peak
        total[h] = jnp.sum(expo, axis=-1, keepdims=True)
        owin[h] = dot_nn(expo.astype(BF16), v)
        qb = qb_ref[...]
        mine = jnp.where(blane == h, 1.0, 0.0).astype(BF16)
        w = dot_nt(qb * mine, kb_ref[...]) * (1.0 / math.sqrt(FD))
        kern = jnp.where(col <= row, 1.0 + w + w * w * 0.5, 0.0).astype(BF16)
        lin[h] = dot_nn(kern, v)
        pick_a = jnp.where(qfirst == h * FD, 1.0, 0.0).astype(BF16)
        pick_b = jnp.where(qsecond == h * FD, 1.0, 0.0).astype(BF16)
        a = dot_nn(qb, pick_a) + qone_a
        b = dot_nn(qb, pick_b) + qone_b
        qfeat[h] = (a * b * qscale).astype(BF16)

    for fetch in fetches[2:]:
        fetch.wait()
    each_head(local)

    @pl.when(me > early)
    def _():
        each_head(chain)

    reach = jnp.where(has_prev, 0, tokens)

    def finish(h):
        scores = dot_nt(q_ref[:, cols(h)], khalo[h]) * root
        scores = jnp.where(col >= row + reach, scores, NEG)
        before = top[h]
        peak = jnp.maximum(before, jnp.max(scores, axis=-1, keepdims=True))
        expo = jnp.exp(scores - peak)
        shrink = jnp.exp(before - peak)
        full = total[h] * shrink + jnp.sum(expo, axis=-1, keepdims=True)
        window = (owin[h] * shrink + dot_nn(expo.astype(BF16), vhalo[h])) / full
        raw = lin[h] + dot_nn(qfeat[h], prior[h].astype(BF16))
        inv = lax.rsqrt(jnp.mean(raw * raw, axis=-1, keepdims=True) + 1e-05)
        out_ref[:, cols(h)] = (window + raw * inv * gain_ref[:, cols(h)]).astype(BF16)

    group = 2
    for begin in range(0, heads, group):
        members = range(begin, min(begin + group, heads))

        @pl.when(has_prev)
        def _():
            for h in members:
                kcopy(h).wait_recv()
                vcopy(h).wait_recv()

        for h in members:
            finish(h)

    @pl.when(has_next)
    def _():
        def sent(h):
            kcopy(h).wait_send()
            vcopy(h).wait_send()
            pcopy(h).wait_send()
        each_head(sent)


def solution(mesh):
    n = mesh.shape["seq"]
    carried = BF16 if n <= 16 else F32

    def on_device(queries, key_rows, value_rows, query_basis, key_basis, linear_gain):
        tokens, width = queries.shape
        heads = width // DH
        vmem = pl.BlockSpec(memory_space=pltpu.VMEM)
        dma = pltpu.SemaphoreType.DMA((heads,))
        flops = 2 * tokens * heads * DH * (4 * tokens + tokens + 2 * ROWS + 4 * ROWS)
        return pl.pallas_call(
            functools.partial(kernel, n, heads),
            out_shape=jax.ShapeDtypeStruct((tokens, width), BF16),
            in_specs=[pl.BlockSpec(memory_space=pltpu.HBM)] * 6,
            out_specs=vmem,
            scratch_shapes=[
                pltpu.VMEM((tokens, width), BF16),
                pltpu.VMEM((tokens, width), BF16),
                pltpu.VMEM((tokens, width), BF16),
                pltpu.VMEM(query_basis.shape, BF16),
                pltpu.VMEM(key_basis.shape, BF16),
                pltpu.VMEM((1, width), F32),
                pltpu.SemaphoreType.DMA((6,)),
                pltpu.VMEM((heads, tokens, DH), BF16),
                pltpu.VMEM((heads, tokens, DH), BF16),
                pltpu.VMEM((heads, ROWS, DH), carried),
                pltpu.VMEM((heads, ROWS, DH), carried),
                pltpu.VMEM((heads, ROWS, DH), F32),
                pltpu.VMEM((heads, tokens, ROWS), BF16),
                pltpu.VMEM((heads, tokens, 1), F32),
                pltpu.VMEM((heads, tokens, 1), F32),
                pltpu.VMEM((heads, tokens, DH), F32),
                pltpu.VMEM((heads, tokens, DH), F32),
                dma, dma, dma, dma, dma, dma,
            ],
            compiler_params=pltpu.CompilerParams(
                collective_id=0, has_side_effects=True, vmem_limit_bytes=40 * 2**20),
            cost_estimate=pl.CostEstimate(
                flops=flops, bytes_accessed=8 * tokens * width, transcendentals=2 * tokens * tokens * heads),
        )(queries, key_rows, value_rows, query_basis, key_basis, linear_gain.reshape(1, width))

    rows = P(("groups", "seq"), "heads")
    return jax.shard_map(
        on_device,
        mesh=mesh,
        in_specs=(rows, rows, rows, rows, rows, P("heads")),
        out_specs=rows,
        check_vma=False,
    )
```

```python
import functools
import math

import jax
import jax.numpy as jnp
from jax import lax
from jax.experimental import pallas as pl
from jax.experimental.pallas import tpu as pltpu
from jax.sharding import PartitionSpec as P

DH = 128
FD = 16
ROWS = 160
ONE = 136
LIN = 144
NEG = -1e30
F32 = jnp.float32
BF16 = jnp.bfloat16


def dot_nn(a, b):
    return lax.dot_general(a, b, (((1,), (0,)), ((), ())), preferred_element_type=F32)


def dot_nt(a, b):
    return lax.dot_general(a, b, (((1,), (1,)), ((), ())), preferred_element_type=F32)


def pair_places(c):
    i = c % FD
    j = (i + c // FD) % FD
    return i, j


def entry_scale(c, doubled):
    pair = 0.25 / math.sqrt(2.0)
    off = 2.0 * pair if doubled else pair
    scale = jnp.where(c < FD, pair, off)
    scale = jnp.where(c >= ONE, 0.0, scale)
    scale = jnp.where(c == ONE, 1.0, scale)
    return jnp.where(c >= LIN, 0.5, scale).astype(F32)


def kernel(n, heads, q_hbm, k_hbm, v_hbm, qb_hbm, kb_hbm, gain_hbm, out_ref,
           q_ref, k_ref, v_ref, qb_ref, kb_ref, gain_ref, loads, khalo, vhalo, prior, onward, state, qfeat, top, total, owin, lin,
           ksend, vsend, psend, krecv, vrecv, precv):
    me = lax.axis_index("seq")
    tokens = q_ref.shape[0]
    has_next = me < n - 1
    has_prev = me > 0
    nxt = {"seq": jnp.minimum(me + 1, n - 1)}
    prv = {"seq": jnp.maximum(me - 1, 0)}

    pairs = ((kb_hbm, kb_ref), (v_hbm, v_ref), (k_hbm, k_ref), (qb_hbm, qb_ref), (q_hbm, q_ref),
             (gain_hbm, gain_ref))
    fetches = [pltpu.make_async_copy(a, b, loads.at[at]) for at, (a, b) in enumerate(pairs)]
    barrier = pltpu.get_barrier_semaphore()

    @pl.when(has_prev)
    def _():
        pl.semaphore_signal(barrier, inc=1, device_id=prv, device_id_type=pl.DeviceIdType.MESH)

    for fetch in fetches:
        fetch.start()

    @pl.when(me == 0)
    def _():
        khalo[...] = jnp.zeros_like(khalo)
        vhalo[...] = jnp.zeros_like(vhalo)
        prior[...] = jnp.zeros_like(prior)

    @pl.when(has_next)
    def _():
        pl.semaphore_wait(barrier, 1)

    def cols(h):
        return pl.ds(h * DH, DH)

    def kcopy(h):
        return pltpu.make_async_remote_copy(
            src_ref=k_hbm.at[:, cols(h)], dst_ref=khalo.at[h], send_sem=ksend.at[h],
            recv_sem=krecv.at[h], device_id=nxt, device_id_type=pl.DeviceIdType.MESH)

    def vcopy(h):
        return pltpu.make_async_remote_copy(
            src_ref=v_hbm.at[:, cols(h)], dst_ref=vhalo.at[h], send_sem=vsend.at[h],
            recv_sem=vrecv.at[h], device_id=nxt, device_id_type=pl.DeviceIdType.MESH)

    def pcopy(h):
        return pltpu.make_async_remote_copy(
            src_ref=onward.at[h], dst_ref=prior.at[h], send_sem=psend.at[h],
            recv_sem=precv.at[h], device_id=nxt, device_id_type=pl.DeviceIdType.MESH)

    def each_head(body):
        for h in range(heads):
            body(h)

    crow = lax.broadcasted_iota(jnp.int32, (ROWS, heads * FD), 0)
    lane = lax.broadcasted_iota(jnp.int32, (ROWS, heads * FD), 1)
    i, j = pair_places(crow)
    first = jnp.where(crow == ONE, -1, lane - i)
    second = jnp.where(crow >= ONE, -1, lane - j)
    ccol = lax.broadcasted_iota(jnp.int32, (ROWS, 1), 0)
    kscale = entry_scale(ccol, False)
    kone_a = jnp.where(ccol == ONE, 1.0, 0.0).astype(F32)
    kone_b = jnp.where(ccol >= ONE, 1.0, 0.0).astype(F32)

    def own_state(h):
        pick_a = jnp.where(first == h * FD, 1.0, 0.0).astype(BF16)
        pick_b = jnp.where(second == h * FD, 1.0, 0.0).astype(BF16)
        a = dot_nt(pick_a, kb_ref[...]) + kone_a
        b = dot_nt(pick_b, kb_ref[...]) + kone_b
        feats = (a * b * kscale).astype(BF16)
        state[h] = dot_nn(feats, v_ref[:, cols(h)])

    ahead = me - 1

    def send_halo(h, now):
        @pl.when(has_next & now)
        def _():
            kcopy(h).start()
            vcopy(h).start()

    for h in range(heads):
        send_halo(h, h < ahead)

    fetches[0].wait()
    fetches[1].wait()
    for begin in range(0, heads, 4):
        members = range(begin, min(begin + 4, heads))
        for h in members:
            own_state(h)

        @pl.when((me == 0) & has_next)
        def _():
            for h in members:
                onward[h] = state[h].astype(onward.dtype)
                pcopy(h).start()

    @pl.when(me == 0)
    def _():
        for h in range(heads):
            send_halo(h, True)

    def chain(h):
        pcopy(h).wait_recv()

        @pl.when(has_next)
        def _():
            onward[h] = (prior[h].astype(F32) + state[h]).astype(onward.dtype)
            pcopy(h).start()

    early = n // 2 - 1

    @pl.when(has_prev & (me <= early))
    def _():
        each_head(chain)
        for h in range(heads):
            send_halo(h, h >= ahead)

    row = lax.broadcasted_iota(jnp.int32, (tokens, tokens), 0)
    col = lax.broadcasted_iota(jnp.int32, (tokens, tokens), 1)
    qrow = lax.broadcasted_iota(jnp.int32, (heads * FD, ROWS), 1)
    qlane = lax.broadcasted_iota(jnp.int32, (heads * FD, ROWS), 0)
    qi, qj = pair_places(qrow)
    qfirst = jnp.where(qrow == ONE, -1, qlane - qi)
    qsecond = jnp.where(qrow >= ONE, -1, qlane - qj)
    clane = lax.broadcasted_iota(jnp.int32, (1, ROWS), 1)
    qscale = entry_scale(clane, True)
    qone_a = jnp.where(clane == ONE, 1.0, 0.0).astype(F32)
    qone_b = jnp.where(clane >= ONE, 1.0, 0.0).astype(F32)
    blane = lax.broadcasted_iota(jnp.int32, (1, heads * FD), 1) // FD
    root = 1.0 / math.sqrt(DH)

    def local(h):
        v = v_ref[:, cols(h)]
        scores = dot_nt(q_ref[:, cols(h)], k_ref[:, cols(h)]) * root
        scores = jnp.where(col <= row, scores, NEG)
        peak = jnp.max(scores, axis=-1, keepdims=True)
        expo = jnp.exp(scores - peak)
        top[h] = peak
        total[h] = jnp.sum(expo, axis=-1, keepdims=True)
        owin[h] = dot_nn(expo.astype(BF16), v)
        qb = qb_ref[...]
        mine = jnp.where(blane == h, 1.0, 0.0).astype(BF16)
        w = dot_nt(qb * mine, kb_ref[...]) * (1.0 / math.sqrt(FD))
        kern = jnp.where(col <= row, 1.0 + w + w * w * 0.5, 0.0).astype(BF16)
        lin[h] = dot_nn(kern, v)
        pick_a = jnp.where(qfirst == h * FD, 1.0, 0.0).astype(BF16)
        pick_b = jnp.where(qsecond == h * FD, 1.0, 0.0).astype(BF16)
        a = dot_nn(qb, pick_a) + qone_a
        b = dot_nn(qb, pick_b) + qone_b
        qfeat[h] = (a * b * qscale).astype(BF16)

    for fetch in fetches[2:]:
        fetch.wait()
    each_head(local)

    @pl.when(me > early)
    def _():
        each_head(chain)
        for h in range(heads):
            send_halo(h, h >= ahead)

    reach = jnp.where(has_prev, 0, tokens)

    def finish(h):
        scores = dot_nt(q_ref[:, cols(h)], khalo[h]) * root
        scores = jnp.where(col >= row + reach, scores, NEG)
        before = top[h]
        peak = jnp.maximum(before, jnp.max(scores, axis=-1, keepdims=True))
        expo = jnp.exp(scores - peak)
        shrink = jnp.exp(before - peak)
        full = total[h] * shrink + jnp.sum(expo, axis=-1, keepdims=True)
        window = (owin[h] * shrink + dot_nn(expo.astype(BF16), vhalo[h])) / full
        raw = lin[h] + dot_nn(qfeat[h], prior[h].astype(BF16))
        inv = lax.rsqrt(jnp.mean(raw * raw, axis=-1, keepdims=True) + 1e-05)
        out_ref[:, cols(h)] = (window + raw * inv * gain_ref[:, cols(h)]).astype(BF16)

    group = 2
    for begin in range(0, heads, group):
        members = range(begin, min(begin + group, heads))

        @pl.when(has_prev)
        def _():
            for h in members:
                kcopy(h).wait_recv()
                vcopy(h).wait_recv()

        for h in members:
            finish(h)

    @pl.when(has_next)
    def _():
        def sent(h):
            kcopy(h).wait_send()
            vcopy(h).wait_send()
            pcopy(h).wait_send()
        each_head(sent)


def solution(mesh):
    n = mesh.shape["seq"]
    carried = BF16 if n <= 16 else F32

    def on_device(queries, key_rows, value_rows, query_basis, key_basis, linear_gain):
        tokens, width = queries.shape
        heads = width // DH
        vmem = pl.BlockSpec(memory_space=pltpu.VMEM)
        dma = pltpu.SemaphoreType.DMA((heads,))
        flops = 2 * tokens * heads * DH * (4 * tokens + tokens + 2 * ROWS + 4 * ROWS)
        return pl.pallas_call(
            functools.partial(kernel, n, heads),
            out_shape=jax.ShapeDtypeStruct((tokens, width), BF16),
            in_specs=[pl.BlockSpec(memory_space=pltpu.HBM)] * 6,
            out_specs=vmem,
            scratch_shapes=[
                pltpu.VMEM((tokens, width), BF16),
                pltpu.VMEM((tokens, width), BF16),
                pltpu.VMEM((tokens, width), BF16),
                pltpu.VMEM(query_basis.shape, BF16),
                pltpu.VMEM(key_basis.shape, BF16),
                pltpu.VMEM((1, width), F32),
                pltpu.SemaphoreType.DMA((6,)),
                pltpu.VMEM((heads, tokens, DH), BF16),
                pltpu.VMEM((heads, tokens, DH), BF16),
                pltpu.VMEM((heads, ROWS, DH), carried),
                pltpu.VMEM((heads, ROWS, DH), carried),
                pltpu.VMEM((heads, ROWS, DH), F32),
                pltpu.VMEM((heads, tokens, ROWS), BF16),
                pltpu.VMEM((heads, tokens, 1), F32),
                pltpu.VMEM((heads, tokens, 1), F32),
                pltpu.VMEM((heads, tokens, DH), F32),
                pltpu.VMEM((heads, tokens, DH), F32),
                dma, dma, dma, dma, dma, dma,
            ],
            compiler_params=pltpu.CompilerParams(
                collective_id=0, has_side_effects=True, vmem_limit_bytes=63 * 2**20),
            cost_estimate=pl.CostEstimate(
                flops=flops, bytes_accessed=8 * tokens * width, transcendentals=2 * tokens * tokens * heads),
        )(queries, key_rows, value_rows, query_basis, key_basis, linear_gain.reshape(1, width))

    rows = P(("groups", "seq"), "heads")
    return jax.shard_map(
        on_device,
        mesh=mesh,
        in_specs=(rows, rows, rows, rows, rows, P("heads")),
        out_specs=rows,
        check_vma=False,
    )
```

```python
import functools
import math

import jax
import jax.numpy as jnp
from jax import lax
from jax.experimental import pallas as pl
from jax.experimental.pallas import tpu as pltpu
from jax.sharding import PartitionSpec as P

DH = 128
FD = 16
ROWS = 160
ONE = 136
LIN = 144
NEG = -1e30
F32 = jnp.float32
BF16 = jnp.bfloat16


def dot_nn(a, b):
    return lax.dot_general(a, b, (((1,), (0,)), ((), ())), preferred_element_type=F32)


def dot_nt(a, b):
    return lax.dot_general(a, b, (((1,), (1,)), ((), ())), preferred_element_type=F32)


def pair_places(c):
    i = c % FD
    j = (i + c // FD) % FD
    return i, j


def entry_scale(c, doubled):
    pair = 0.25 / math.sqrt(2.0)
    off = 2.0 * pair if doubled else pair
    scale = jnp.where(c < FD, pair, off)
    scale = jnp.where(c >= ONE, 0.0, scale)
    scale = jnp.where(c == ONE, 1.0, scale)
    return jnp.where(c >= LIN, 0.5, scale).astype(F32)


def kernel(n, heads, q_hbm, k_hbm, v_hbm, qb_hbm, kb_hbm, gain_hbm, out_ref,
           q_ref, k_ref, v_ref, qb_ref, kb_ref, gain_ref, loads, khalo, vhalo, bhalo, relay,
           carry, onward, prior, state, qfeat, top, total, owin, lin, bsend, brecv,
           ksend, vsend, psend, krecv, vrecv, precv, rsend, rrecv, fsend):
    me = lax.axis_index("seq")
    tokens = q_ref.shape[0]
    has_next = me < n - 1
    has_prev = me > 0
    even = lax.rem(me, 2) == 0
    has_after = me + 2 < n
    relays = even & has_after
    relayed_out = (~even) & has_next
    relayed = relay.shape[0]
    mesh_ids = pl.DeviceIdType.MESH

    def at(distance):
        return {"seq": jnp.clip(me + distance, 0, n - 1)}

    pairs = ((kb_hbm, kb_ref), (v_hbm, v_ref), (k_hbm, k_ref), (qb_hbm, qb_ref), (q_hbm, q_ref),
             (gain_hbm, gain_ref))
    fetches = [pltpu.make_async_copy(a, b, loads.at[slot]) for slot, (a, b) in enumerate(pairs)]
    barrier = pltpu.get_barrier_semaphore()

    for distance, sends in ((-1, has_prev), (-2, me >= 2), (1, relays)):
        @pl.when(sends)
        def _():
            pl.semaphore_signal(barrier, inc=1, device_id=at(distance), device_id_type=mesh_ids)

    for fetch in fetches:
        fetch.start()

    @pl.when(me == 0)
    def _():
        khalo[...] = jnp.zeros_like(khalo)
        vhalo[...] = jnp.zeros_like(vhalo)
        bhalo[...] = jnp.zeros_like(bhalo)

    @pl.when(me < 2)
    def _():
        carry[...] = jnp.zeros_like(carry)

    @pl.when(has_next)
    def _():
        reached = 1 + has_after.astype(jnp.int32) + relayed_out.astype(jnp.int32)
        pl.semaphore_wait(barrier, reached)

    def cols(h):
        return pl.ds(h * DH, DH)

    def remote(src, dst, send, recv, distance):
        return pltpu.make_async_remote_copy(
            src_ref=src, dst_ref=dst, send_sem=send, recv_sem=recv, device_id=at(distance),
            device_id_type=mesh_ids)

    def bcopy():
        return remote(kb_hbm, bhalo, bsend.at[0], brecv.at[0], 1)

    def kcopy(h):
        return remote(k_hbm.at[:, cols(h)], khalo.at[h], ksend.at[h], krecv.at[h], 1)

    def vcopy(h):
        return remote(v_hbm.at[:, cols(h)], vhalo.at[h], vsend.at[h], vrecv.at[h], 1)

    def pcopy(h):
        return remote(onward.at[h], carry.at[h], psend.at[h], precv.at[h], 2)

    def rcopy(h):
        return remote(k_hbm.at[:, cols(h)], relay.at[h], rsend.at[h], rrecv.at[h], -1)

    def fcopy(h):
        return remote(relay.at[h], khalo.at[h], fsend.at[h], krecv.at[h], 2)

    def each_head(body):
        for h in range(heads):
            body(h)

    @pl.when(has_next)
    def _():
        bcopy().start()

    @pl.when(has_next)
    def _():
        for h in range(heads):
            vcopy(h).start()

    crow = lax.broadcasted_iota(jnp.int32, (ROWS, heads * FD), 0)
    lane = lax.broadcasted_iota(jnp.int32, (ROWS, heads * FD), 1)
    i, j = pair_places(crow)
    first = jnp.where(crow == ONE, -1, lane - i)
    second = jnp.where(crow >= ONE, -1, lane - j)
    ccol = lax.broadcasted_iota(jnp.int32, (ROWS, 1), 0)
    kscale = entry_scale(ccol, False)
    kone_a = jnp.where(ccol == ONE, 1.0, 0.0).astype(F32)
    kone_b = jnp.where(ccol >= ONE, 1.0, 0.0).astype(F32)

    def state_of(h, basis, values):
        pick_a = jnp.where(first == h * FD, 1.0, 0.0).astype(BF16)
        pick_b = jnp.where(second == h * FD, 1.0, 0.0).astype(BF16)
        a = dot_nt(pick_a, basis) + kone_a
        b = dot_nt(pick_b, basis) + kone_b
        feats = (a * b * kscale).astype(BF16)
        return dot_nn(feats, values)

    @pl.when(even & has_next)
    def _():
        for h in range(heads):
            kcopy(h).start()

    @pl.when(relayed_out)
    def _():
        for h in range(relayed):
            rcopy(h).start()

    fetches[0].wait()
    fetches[1].wait()
    for h in range(heads):
        state[h] = state_of(h, kb_ref[...], v_ref[:, cols(h)])

    row = lax.broadcasted_iota(jnp.int32, (tokens, tokens), 0)
    col = lax.broadcasted_iota(jnp.int32, (tokens, tokens), 1)
    qrow = lax.broadcasted_iota(jnp.int32, (heads * FD, ROWS), 1)
    qlane = lax.broadcasted_iota(jnp.int32, (heads * FD, ROWS), 0)
    qi, qj = pair_places(qrow)
    qfirst = jnp.where(qrow == ONE, -1, qlane - qi)
    qsecond = jnp.where(qrow >= ONE, -1, qlane - qj)
    clane = lax.broadcasted_iota(jnp.int32, (1, ROWS), 1)
    qscale = entry_scale(clane, True)
    qone_a = jnp.where(clane == ONE, 1.0, 0.0).astype(F32)
    qone_b = jnp.where(clane >= ONE, 1.0, 0.0).astype(F32)
    blane = lax.broadcasted_iota(jnp.int32, (1, heads * FD), 1) // FD
    root = 1.0 / math.sqrt(DH)

    def local(h):
        v = v_ref[:, cols(h)]
        scores = dot_nt(q_ref[:, cols(h)], k_ref[:, cols(h)]) * root
        scores = jnp.where(col <= row, scores, NEG)
        peak = jnp.max(scores, axis=-1, keepdims=True)
        expo = jnp.exp(scores - peak)
        top[h] = peak
        total[h] = jnp.sum(expo, axis=-1, keepdims=True)
        owin[h] = dot_nn(expo.astype(BF16), v)
        qb = qb_ref[...]
        mine = jnp.where(blane == h, 1.0, 0.0).astype(BF16)
        w = dot_nt(qb * mine, kb_ref[...]) * (1.0 / math.sqrt(FD))
        kern = jnp.where(col <= row, 1.0 + w + w * w * 0.5, 0.0).astype(BF16)
        lin[h] = dot_nn(kern, v)
        pick_a = jnp.where(qfirst == h * FD, 1.0, 0.0).astype(BF16)
        pick_b = jnp.where(qsecond == h * FD, 1.0, 0.0).astype(BF16)
        a = dot_nn(qb, pick_a) + qone_a
        b = dot_nn(qb, pick_b) + qone_b
        qfeat[h] = (a * b * qscale).astype(BF16)

    for fetch in fetches[2:]:
        fetch.wait()
    each_head(local)

    @pl.when(has_prev)
    def _():
        bcopy().wait_recv()

    for h in range(heads):
        @pl.when(has_prev)
        def _():
            vcopy(h).wait_recv()

        between = state_of(h, bhalo[...], vhalo[h])

        @pl.when(me >= 2)
        def _():
            pcopy(h).wait_recv()

        before = carry[h].astype(F32) + between
        prior[h] = before.astype(BF16)

        @pl.when(has_after)
        def _():
            onward[h] = (before + state[h]).astype(onward.dtype)
            pcopy(h).start()

    @pl.when(relays)
    def _():
        for h in range(relayed):
            rcopy(h).wait_recv()
            fcopy(h).start()

    @pl.when(relayed_out)
    def _():
        for h in range(relayed, heads):
            kcopy(h).start()

    reach = jnp.where(has_prev, 0, tokens)

    def finish(h):
        scores = dot_nt(q_ref[:, cols(h)], khalo[h]) * root
        scores = jnp.where(col >= row + reach, scores, NEG)
        before = top[h]
        peak = jnp.maximum(before, jnp.max(scores, axis=-1, keepdims=True))
        expo = jnp.exp(scores - peak)
        shrink = jnp.exp(before - peak)
        full = total[h] * shrink + jnp.sum(expo, axis=-1, keepdims=True)
        window = (owin[h] * shrink + dot_nn(expo.astype(BF16), vhalo[h])) / full
        raw = lin[h] + dot_nn(qfeat[h], prior[h])
        inv = lax.rsqrt(jnp.mean(raw * raw, axis=-1, keepdims=True) + 1e-05)
        out_ref[:, cols(h)] = (window + raw * inv * gain_ref[:, cols(h)]).astype(BF16)

    group = 2
    for begin in range(0, heads, group):
        members = range(begin, min(begin + group, heads))

        @pl.when(has_prev)
        def _():
            for h in members:
                kcopy(h).wait_recv()

        for h in members:
            finish(h)

    @pl.when(has_next)
    def _():
        bcopy().wait_send()
        for h in range(heads):
            vcopy(h).wait_send()
        for h in range(relayed, heads):
            kcopy(h).wait_send()

    @pl.when(even & has_next)
    def _():
        for h in range(relayed):
            kcopy(h).wait_send()

    @pl.when(relayed_out)
    def _():
        for h in range(relayed):
            rcopy(h).wait_send()

    @pl.when(relays)
    def _():
        for h in range(relayed):
            fcopy(h).wait_send()

    @pl.when(has_after)
    def _():
        for h in range(heads):
            pcopy(h).wait_send()


def solution(mesh):
    n = mesh.shape["seq"]
    carried = BF16 if n <= 16 else F32

    def on_device(queries, key_rows, value_rows, query_basis, key_basis, linear_gain):
        tokens, width = queries.shape
        heads = width // DH
        vmem = pl.BlockSpec(memory_space=pltpu.VMEM)
        dma = pltpu.SemaphoreType.DMA((heads,))
        flops = 2 * tokens * heads * DH * (4 * tokens + tokens + 2 * ROWS + 4 * ROWS)
        return pl.pallas_call(
            functools.partial(kernel, n, heads),
            out_shape=jax.ShapeDtypeStruct((tokens, width), BF16),
            in_specs=[pl.BlockSpec(memory_space=pltpu.HBM)] * 6,
            out_specs=vmem,
            scratch_shapes=[
                pltpu.VMEM((tokens, width), BF16),
                pltpu.VMEM((tokens, width), BF16),
                pltpu.VMEM((tokens, width), BF16),
                pltpu.VMEM(query_basis.shape, BF16),
                pltpu.VMEM(key_basis.shape, BF16),
                pltpu.VMEM((1, width), F32),
                pltpu.SemaphoreType.DMA((6,)),
                pltpu.VMEM((heads, tokens, DH), BF16),
                pltpu.VMEM((heads, tokens, DH), BF16),
                pltpu.VMEM(key_basis.shape, BF16),
                pltpu.VMEM((max(heads * 3 // 8, 1), tokens, DH), BF16),
                pltpu.VMEM((heads, ROWS, DH), carried),
                pltpu.VMEM((heads, ROWS, DH), carried),
                pltpu.VMEM((heads, ROWS, DH), BF16),
                pltpu.VMEM((heads, ROWS, DH), F32),
                pltpu.VMEM((heads, tokens, ROWS), BF16),
                pltpu.VMEM((heads, tokens, 1), F32),
                pltpu.VMEM((heads, tokens, 1), F32),
                pltpu.VMEM((heads, tokens, DH), F32),
                pltpu.VMEM((heads, tokens, DH), F32),
                pltpu.SemaphoreType.DMA((1,)),
                pltpu.SemaphoreType.DMA((1,)),
                dma, dma, dma, dma, dma, dma, dma, dma, dma,
            ],
            compiler_params=pltpu.CompilerParams(
                collective_id=0, has_side_effects=True, vmem_limit_bytes=63 * 2**20),
            cost_estimate=pl.CostEstimate(
                flops=flops, bytes_accessed=8 * tokens * width, transcendentals=2 * tokens * tokens * heads),
        )(queries, key_rows, value_rows, query_basis, key_basis, linear_gain.reshape(1, width))

    rows = P(("groups", "seq"), "heads")
    return jax.shard_map(
        on_device,
        mesh=mesh,
        in_specs=(rows, rows, rows, rows, rows, P("heads")),
        out_specs=rows,
        check_vma=False,
    )
```
